32 devices in a mesh: leaf: 8 (over z, y), chan: 4 (over x, core).
Axes of the slice: x: 2, y: 2, z: 4, core: 2. Of those that a mesh axis runs over, the one named last changes fastest.
Arguments:
- features: bfloat16 [64, 32768], P(None, 'leaf'), may hold values from -6 to 6
- neighbours: int32 [27, 32768], P(None, 'leaf'), may hold values from -1 to 2048, as said below
- child_count: int32 [8], P('leaf'), may hold values from 1024 to 4096, as said below
- dest: int32 [4096], P('leaf'), may hold values from -1 to 4095, as said below
- conv_weight: bfloat16 [27, 64, 64], P(None, None, 'chan'), may hold values from -0.15625 to 0.15625
- merge_weight: bfloat16 [8, 64, 128], P(None, None, 'chan'), may hold values from -0.25 to 0.25
- parent_grad: bfloat16 [128, 4096], P('chan', 'leaf'), may hold values from -6 to 6
Outputs:
- parents: bfloat16 [128, 4096], P('chan', 'leaf')
- merge_weight_grad: float32 [8, 64, 128], P(None, None, 'chan')
The draws below stay inside these ranges and needn't reach their ends.
Inputs may be any that keep to these rules, and one draw needn't show every extreme that they name: `neighbours`: entry [k, r] is -1 where the neighbour is empty; else r + entry - 1024 is the index of a valid child octant, so the entry lies in 0 to 2048. Slots beyond a device's valid octants may hold entries too. Row 13 holds 1024 for every valid r. `child_count`: A multiple of 8; the valid child octants are the first ones of each device's 4096 slots; in every draw some device is full. `dest`: for parent slot g of device d, valid where g < child_count[d] / 8: t // 512 is the owner device and t % 512 = d * 64 + g % 64; the 64 slots with one value of g // 64 share an owner, and distinct such blocks of one device have distinct owners; -1 where g is not valid.
All inputs are finite; a program needn't handle non-finite values.
Results may differ from the reference program's by a relative error of at most 0.005.
Values may be sent and summed in bfloat16 or wider, within the bound.
A program may use at most 64 MiB of HBM per device.

```python
import math
import jax
import jax.numpy as jnp
from jax import lax

C1 = 64
C2 = 128
TAPS = 27
KIDS = 8
PG = 512
CHILD = 4096
CAP = 64
HALO = 1024
N_LEAF = 8


def layout(key):
    base_key = jax.random.fold_in(key, 11)
    first_key = jax.random.fold_in(base_key, 1)
    second_key = jax.random.fold_in(base_key, 2)
    third_key = jax.random.fold_in(base_key, 3)
    groups = jax.random.randint(first_key, (N_LEAF,), PG // 4, PG + 1)
    full_device = jax.random.randint(second_key, (), 0, N_LEAF)
    device_ids = jnp.arange(N_LEAF)
    groups = jnp.where((device_ids == full_device) | (device_ids == N_LEAF - 2), PG, groups)
    shifts = jax.random.permutation(third_key, N_LEAF)
    return (groups.astype(jnp.int32), shifts.astype(jnp.int32))


def draw_child_count(key, part):
    groups, shifts = layout(key)
    return (groups * 8).astype(jnp.int32)


def draw_dest(key, part):
    groups, shifts = layout(key)
    slot_ids = jnp.arange(PG, dtype=jnp.int32)
    blocks = slot_ids // CAP
    within = slot_ids % CAP
    devices = jnp.arange(N_LEAF, dtype=jnp.int32)[:, None]
    owners = (devices + shifts[blocks][None, :]) % N_LEAF
    target = owners * PG + devices * CAP + within[None, :]
    living = slot_ids[None, :] < groups[:, None]
    return jnp.where(living, target, -1).reshape(N_LEAF * PG).astype(jnp.int32)


def draw_neighbours(key, part):
    groups, shifts = layout(key)
    counts = groups * 8
    total_rows = N_LEAF * CHILD
    row_ids = jnp.arange(total_rows, dtype=jnp.int32)
    offsets = jax.random.randint(jax.random.fold_in(key, 21), (TAPS, total_rows), -HALO, HALO + 1)
    centre = TAPS // 2
    offsets = offsets.at[centre].set(0)
    target = row_ids[None, :] + offsets
    inside = (target >= 0) & (target < total_rows)
    clipped = jnp.clip(target, 0, total_rows - 1)
    target_dev = clipped // CHILD
    target_loc = clipped - target_dev * CHILD
    living = target_loc < counts[target_dev]
    kept_mask = jax.random.randint(jax.random.fold_in(key, 22), (TAPS, total_rows), 0, 6) != 0
    kept_mask = kept_mask.at[centre].set(True)
    chosen = inside & living & kept_mask
    return jnp.where(chosen, offsets + HALO, -1).astype(jnp.int32)


def levels(key, extent, shards, low, top_value):
    def one(dim, parts):
        heights = jax.random.uniform(jax.random.fold_in(jax.random.fold_in(key, 6), dim), (parts,), jnp.float32, low / len(shards), top_value / len(shards))
        return jnp.repeat(jnp.exp(heights), extent[dim] // parts).reshape((-1,) + (1,) * (len(extent) - dim - 1))

    factor_of = one(*shards[0])
    for cut in shards[1:]:
        factor_of = factor_of * one(*cut)
    return factor_of


def noise(key, shape, deviation, limit, shards=(), kind=jnp.bfloat16):
    level = levels(key, shape, shards, -0.22, 0.18) if shards else 1.0
    drawn = jax.random.normal(key, shape, jnp.float32) * deviation * level
    return jnp.minimum(jnp.maximum(drawn, -limit), limit).astype(kind)


def setup_inputs(seed: int = 0) -> dict:
    arg_keys = jax.random.split(jax.random.key(seed), 8)
    return {
        "features": noise(arg_keys[0], (C1, N_LEAF * CHILD), 1.0, 6.0, ((1, 8),)),
        "neighbours": draw_neighbours(jax.random.fold_in(arg_keys[7], 71), 0),
        "child_count": draw_child_count(jax.random.fold_in(arg_keys[7], 71), 0),
        "dest": draw_dest(jax.random.fold_in(arg_keys[7], 71), 0),
        "conv_weight": noise(arg_keys[4], (TAPS, C1, C1), (TAPS * C1) ** -0.5, 0.15625, ((2, 4),)),
        "merge_weight": noise(arg_keys[5], (KIDS, C1, C2), (KIDS * C1) ** -0.5, 0.25, ((2, 4),)),
        "parent_grad": noise(arg_keys[6], (C2, N_LEAF * PG), 1.0, 6.0, ((0, 4), (1, 8))),
    }


def reference(features, neighbours, child_count, dest, conv_weight, merge_weight, parent_grad):
    conv_full = conv_weight.astype(jnp.float32)

    def device_block(device):
        offset_block = lax.dynamic_slice_in_dim(neighbours, device * CHILD, CHILD, 1)
        present = offset_block >= 0
        row_ids = device * CHILD + jnp.arange(CHILD, dtype=jnp.int32)
        global_index = row_ids[None, :] + offset_block - HALO
        safe_index = jnp.where(present, global_index, 0).astype(jnp.int32)
        gathered = features[:, safe_index] * present.astype(jnp.bfloat16)[None]
        pre_act = jnp.einsum('ckr,kco->or', gathered.astype(jnp.float32), conv_full)
        living = jnp.arange(CHILD, dtype=jnp.int32) < child_count[device]
        return (jnp.maximum(pre_act, 0.0) * living[None, :]).astype(jnp.bfloat16)
    stacked = lax.map(device_block, jnp.arange(N_LEAF, dtype=jnp.int32))
    hidden = jnp.moveaxis(stacked, 0, 1).reshape(C1, N_LEAF * CHILD)
    grouped = hidden.reshape(C1, N_LEAF * PG, KIDS).astype(jnp.float32)
    merged = jnp.einsum('cqk,kco->oq', grouped, merge_weight.astype(jnp.float32)).astype(jnp.bfloat16)
    living_group = dest >= 0
    slot_place = jnp.where(living_group, dest, N_LEAF * PG)
    parents = jnp.zeros((C2, N_LEAF * PG), jnp.bfloat16).at[:, slot_place].set(merged, mode='drop')
    fetched = parent_grad[:, jnp.where(living_group, dest, 0)] * living_group.astype(jnp.bfloat16)[None, :]
    weight_term = jnp.einsum('cqk,oq->kco', grouped, fetched.astype(jnp.float32))
    merge_weight_grad = weight_term / math.sqrt(KIDS * PG)
    return (parents, merge_weight_grad)
```

```python
import math

import jax
import jax.numpy as jnp
from jax import lax
from jax.experimental import pallas as pl
from jax.experimental.pallas import tpu as pltpu
from jax.sharding import PartitionSpec as P

KIDS = 8
HALO = 1024
LO = 256
BLOCK = 256
REACH = (2 * HALO + BLOCK) // LO


def subtree_kernel(window, offsets, alive, conv, merge, fetched, merged, grad, picked, hidden, stacked):
    taps, rows = offsets.shape
    width = conv.shape[0]
    groups = rows // KIDS
    slot = lax.broadcasted_iota(jnp.int32, (LO, BLOCK), 0).astype(jnp.float32).astype(jnp.bfloat16)
    local = lax.broadcasted_iota(jnp.int32, (1, BLOCK), 1)
    for block in range(rows // BLOCK):
        span = pl.ds(block * BLOCK, BLOCK)
        source = window[pl.ds(block * width, REACH * width), :]
        for tap in range(taps):
            offset = offsets[pl.ds(tap, 1), span]
            place = local + offset
            chunk = place // LO
            inner = jnp.where(offset >= 0, place - chunk * LO, -1)
            inner = inner.astype(jnp.float32).astype(jnp.bfloat16)
            hot = jnp.where(slot == inner, jnp.bfloat16(1), jnp.bfloat16(0))
            found = jnp.dot(source, hot, preferred_element_type=jnp.float32)
            taken = found[:width]
            for high in range(1, REACH):
                taken = jnp.where(chunk == high, found[high * width : (high + 1) * width], taken)
            picked[pl.ds(tap * width, width), :] = taken.astype(jnp.bfloat16)
        pre_act = jnp.dot(conv[...], picked[...], preferred_element_type=jnp.float32)
        kept = jnp.maximum(pre_act, 0.0) * alive[:, span]
        hidden[:, span] = kept.astype(jnp.bfloat16)
    source_row = lax.broadcasted_iota(jnp.int32, (rows, groups), 0)
    group_row = lax.broadcasted_iota(jnp.int32, (rows, groups), 1) * KIDS
    for kid in range(KIDS):
        order = jnp.where(source_row == group_row + kid, 1.0, 0.0).astype(jnp.bfloat16)
        sorted_kid = jnp.dot(hidden[...], order, preferred_element_type=jnp.float32)
        stacked[pl.ds(kid * width, width), :] = sorted_kid.astype(jnp.bfloat16)
    merged[...] = jnp.dot(merge[...], stacked[...], preferred_element_type=jnp.float32).astype(
        jnp.bfloat16
    )
    grad[...] = lax.dot_general(
        stacked[...], fetched[...], (((1,), (1,)), ((), ())), preferred_element_type=jnp.float32
    )


def passed_along(value, axis, steps):
    count = lax.axis_size(axis)
    initial, last = (max(0, -steps), min(count, count - steps))
    return lax.ppermute(value, axis, [(source, source + steps) for source in range(initial, last)])


def per_device(features, neighbours, child_count, dest, conv_weight, merge_weight, parent_grad):
    row_count = features.shape[1]
    in_width = features.shape[0]
    taps = neighbours.shape[0]
    out_merge = merge_weight.shape[2]
    group_count = row_count // KIDS
    peer_count = lax.axis_size("leaf")
    chan_count = lax.axis_size("chan")
    pair_slots = group_count // peer_count
    valid_rows = child_count[0]
    quarter = row_count // chan_count
    first_global = lax.axis_index("chan") * quarter
    before = passed_along(features[:, row_count - HALO :], "leaf", 1)
    after = passed_along(features[:, :HALO], "leaf", -1)
    extended = jnp.concatenate([before, features, after], axis=1)
    window = lax.dynamic_slice_in_dim(extended, first_global, quarter + 2 * HALO, 1)
    window = window.reshape(in_width, -1, LO).swapaxes(0, 1).reshape(-1, LO)
    offsets = lax.dynamic_slice_in_dim(neighbours, first_global, quarter, 1)
    conv_all = lax.all_gather(conv_weight, "chan", axis=2, tiled=True)
    merge_all = lax.all_gather(merge_weight, "chan", axis=2, tiled=True)
    conv_rows = conv_all.reshape(taps * in_width, in_width).T
    merge_rows = merge_all.reshape(KIDS * in_width, -1).T
    living_rows = first_global + jnp.arange(quarter, dtype=jnp.int32)[None, :] < valid_rows
    alive = living_rows.astype(jnp.float32)

    living_group = dest >= 0
    owner_dev = jnp.where(living_group, dest // group_count, 0)
    within = dest % pair_slots
    target_owner = jnp.where(living_group, owner_dev, peer_count)
    returned = lax.all_to_all(
        parent_grad.reshape(out_merge, peer_count, pair_slots),
        "leaf",
        split_axis=1,
        concat_axis=1,
        tiled=True,
    )
    fetched = returned[:, owner_dev, within] * living_group.astype(jnp.bfloat16)[None, :]
    fetched_rows = lax.all_to_all(fetched, "chan", split_axis=1, concat_axis=0, tiled=True)

    whole = pl.BlockSpec(memory_space=pltpu.VMEM)
    all_merge = out_merge * chan_count
    merged_rows, weight_full = pl.pallas_call(
        subtree_kernel,
        out_shape=(
            jax.ShapeDtypeStruct((all_merge, quarter // KIDS), jnp.bfloat16),
            jax.ShapeDtypeStruct((KIDS * in_width, all_merge), jnp.float32),
        ),
        in_specs=[whole] * 6,
        out_specs=(whole, whole),
        scratch_shapes=[
            pltpu.VMEM((taps * in_width, BLOCK), jnp.bfloat16),
            pltpu.VMEM((in_width, quarter), jnp.bfloat16),
            pltpu.VMEM((KIDS * in_width, quarter // KIDS), jnp.bfloat16),
        ],
        compiler_params=pltpu.CompilerParams(vmem_limit_bytes=40 * 1024 * 1024),
    )(window, offsets, alive, conv_rows, merge_rows, fetched_rows)

    merged = lax.all_to_all(merged_rows, "chan", split_axis=0, concat_axis=1, tiled=True)
    outbox = jnp.zeros((out_merge, peer_count, pair_slots), jnp.bfloat16)
    outbox = outbox.at[:, target_owner, within].set(merged, mode="drop")
    arrived = lax.all_to_all(outbox, "leaf", split_axis=1, concat_axis=1, tiled=True)
    parents = arrived.reshape(out_merge, group_count)
    weight_full = weight_full.reshape(KIDS, in_width, all_merge)
    weight_term = lax.psum_scatter(weight_full, "chan", scatter_dimension=2, tiled=True)
    merge_weight_grad = lax.psum(weight_term, "leaf") / math.sqrt(KIDS * group_count)
    return (parents, merge_weight_grad)


def solution(mesh):
    in_specs = (
        P(None, "leaf"),
        P(None, "leaf"),
        P("leaf"),
        P("leaf"),
        P(None, None, "chan"),
        P(None, None, "chan"),
        P("chan", "leaf"),
    )
    out_specs = (P("chan", "leaf"), P(None, None, "chan"))
    return jax.shard_map(
        per_device, mesh=mesh, in_specs=in_specs, out_specs=out_specs, check_vma=False
    )
```

```python
import functools
import math

import jax
import jax.numpy as jnp
from jax import lax
from jax.experimental import pallas as pl
from jax.experimental.pallas import tpu as pltpu
from jax.sharding import PartitionSpec as P

KIDS = 8
HALO = 1024
LO = 256
BLOCK = 256
REACH = (2 * HALO + BLOCK) // LO
LANES = 128
PIECE_ROWS = 16
MESH = pl.DeviceIdType.MESH


def each(count, step):
    if count <= 8:
        for turn in range(count):
            step(turn)
    else:
        lax.fori_loop(0, count, lambda turn, _: (step(turn), 0)[1], 0)


def octree_kernel(
    chans,
    leaves,
    features,
    neighbours,
    child_count,
    dest,
    conv_own,
    merge_own,
    cotangent,
    parents,
    grad,
    window,
    offsets,
    conv,
    merge,
    backward,
    fetched_out,
    fetched,
    picked,
    hidden,
    stacked,
    merged_out,
    merged,
    outbox,
    inbox,
    part,
    part_in,
    piece,
    piece_in,
    total,
    local_sem,
    halo_send,
    halo_recv,
    conv_send,
    conv_recv,
    merge_send,
    merge_recv,
    back_send,
    back_recv,
    fetched_send,
    fetched_recv,
    merged_send,
    merged_recv,
    box_send,
    box_recv,
    part_send,
    part_recv,
    piece_send,
    piece_recv,
    total_send,
    total_recv,
):
    leaf = lax.axis_index("leaf")
    chan = lax.axis_index("chan")
    width, row_count = features.shape
    taps = neighbours.shape[0]
    quarter = row_count // chans
    groups = quarter // KIDS
    group_count = row_count // KIDS
    pair_slots = group_count // leaves
    out_own = merge_own.shape[0]
    pieces = piece.shape[0]
    first_row = pl.multiple_of(chan * quarter, LO)

    def chan_copy(src, dst, send, recv, turn):
        peer = lax.rem(chan + turn + 1, chans)
        return pltpu.make_async_remote_copy(
            src_ref=src(peer), dst_ref=dst.at[chan], send_sem=send.at[turn],
            recv_sem=recv.at[chan], device_id=(leaf, peer), device_id_type=MESH,
        )

    def chan_arrival(dst, send, recv, turn):
        peer = lax.rem(chan + turn + 1, chans)
        return pltpu.make_async_remote_copy(
            src_ref=dst.at[peer], dst_ref=dst.at[peer], send_sem=send.at[turn],
            recv_sem=recv.at[peer], device_id=(leaf, peer), device_id_type=MESH,
        )

    def leaf_copy(src, dst, send, recv, turn):
        peer = lax.rem(leaf + turn + 1, leaves)
        return pltpu.make_async_remote_copy(
            src_ref=src(peer), dst_ref=dst.at[leaf], send_sem=send.at[turn],
            recv_sem=recv.at[leaf], device_id=(peer, chan), device_id_type=MESH,
        )

    def leaf_arrival(dst, send, recv, turn):
        peer = lax.rem(leaf + turn + 1, leaves)
        return pltpu.make_async_remote_copy(
            src_ref=dst.at[peer], dst_ref=dst.at[peer], send_sem=send.at[turn],
            recv_sem=recv.at[peer], device_id=(peer, chan), device_id_type=MESH,
        )

    def near(at, size):
        return features.at[:, pl.ds(at, size)]

    left_local = pltpu.make_async_copy(
        near(pl.multiple_of(jnp.maximum(first_row - HALO, 0), LO), HALO),
        window.at[:, pl.ds(0, HALO)], local_sem.at[0],
    )
    right_local = pltpu.make_async_copy(
        near(pl.multiple_of(jnp.minimum(first_row + quarter, row_count - HALO), LO), HALO),
        window.at[:, pl.ds(HALO + quarter, HALO)], local_sem.at[1],
    )
    centre_local = pltpu.make_async_copy(
        near(first_row, quarter), window.at[:, pl.ds(HALO, quarter)], local_sem.at[2]
    )
    offsets_local = pltpu.make_async_copy(
        neighbours.at[:, pl.ds(first_row, quarter)], offsets, local_sem.at[3]
    )
    from_left = pltpu.make_async_remote_copy(
        src_ref=near(row_count - HALO, HALO), dst_ref=window.at[:, pl.ds(0, HALO)],
        send_sem=halo_send.at[0], recv_sem=halo_recv.at[0],
        device_id=(jnp.minimum(leaf + 1, leaves - 1), chan), device_id_type=MESH,
    )
    from_right = pltpu.make_async_remote_copy(
        src_ref=near(0, HALO), dst_ref=window.at[:, pl.ds(HALO + quarter, HALO)],
        send_sem=halo_send.at[1], recv_sem=halo_recv.at[1],
        device_id=(jnp.maximum(leaf - 1, 0), chan), device_id_type=MESH,
    )
    at_first = chan == 0
    at_last = chan == chans - 1

    offsets_local.start()
    centre_local.start()
    pl.when(jnp.logical_not(at_first))(left_local.start)
    pl.when(jnp.logical_not(at_last))(right_local.start)

    barrier = pltpu.get_barrier_semaphore()

    def greet_chan(turn):
        peer = lax.rem(chan + turn + 1, chans)
        pl.semaphore_signal(barrier, inc=1, device_id=(leaf, peer), device_id_type=MESH)

    def greet_leaf(turn):
        peer = lax.rem(leaf + turn + 1, leaves)
        pl.semaphore_signal(barrier, inc=1, device_id=(peer, chan), device_id_type=MESH)

    each(chans - 1, greet_chan)
    each(leaves - 1, greet_leaf)
    pl.semaphore_wait(barrier, chans + leaves - 2)

    pl.when(at_first & (leaf < leaves - 1))(from_left.start)
    pl.when(at_last & (leaf > 0))(from_right.start)
    sends = []

    def send_chan(src, dst, send, recv):
        each(chans - 1, lambda turn: chan_copy(src, dst, send, recv, turn).start())
        sends.append((chans - 1, lambda turn: chan_copy(src, dst, send, recv, turn).wait_send()))

    def send_leaf(src, dst, send, recv):
        each(leaves - 1, lambda turn: leaf_copy(src, dst, send, recv, turn).start())
        sends.append((leaves - 1, lambda turn: leaf_copy(src, dst, send, recv, turn).wait_send()))

    def take_chan(dst, send, recv):
        each(chans - 1, lambda turn: chan_arrival(dst, send, recv, turn).wait_recv())

    def take_leaf(dst, send, recv):
        each(leaves - 1, lambda turn: leaf_arrival(dst, send, recv, turn).wait_recv())

    send_chan(lambda peer: conv_own, conv, conv_send, conv_recv)
    send_leaf(lambda peer: cotangent.at[peer], backward, back_send, back_recv)
    send_chan(lambda peer: merge_own, merge, merge_send, merge_recv)
    conv[chan] = conv_own[...]
    merge[chan] = merge_own[...]
    backward[leaf] = cotangent[leaf]

    @pl.when(at_first & (leaf == 0))
    def _():
        window[:, :HALO] = jnp.zeros((width, HALO), jnp.bfloat16)

    @pl.when(at_last & (leaf == leaves - 1))
    def _():
        window[:, HALO + quarter :] = jnp.zeros((width, HALO), jnp.bfloat16)

    offsets_local.wait()
    centre_local.wait()
    pl.when(jnp.logical_not(at_first))(left_local.wait)
    pl.when(jnp.logical_not(at_last))(right_local.wait)
    pl.when(at_first & (leaf > 0))(from_left.wait_recv)
    pl.when(at_last & (leaf < leaves - 1))(from_right.wait_recv)

    slot = lax.broadcasted_iota(jnp.int32, (LO, BLOCK), 0).astype(jnp.float32).astype(jnp.bfloat16)
    local = lax.broadcasted_iota(jnp.int32, (1, BLOCK), 1)
    count = child_count[0]

    def pick(block):
        span = pl.ds(block * BLOCK, BLOCK)
        source = jnp.concatenate(
            [window[:, pl.ds((block + high) * LO, LO)] for high in range(REACH)], axis=0
        )

        def one(tap, _):
            offset = offsets[pl.ds(tap, 1), span]
            place = local + offset
            chunk = place // LO
            inner = jnp.where(offset >= 0, place - chunk * LO, -1)
            inner = inner.astype(jnp.float32).astype(jnp.bfloat16)
            hot = jnp.where(slot == inner, jnp.bfloat16(1), jnp.bfloat16(0))
            found = jnp.dot(source, hot, preferred_element_type=jnp.float32)
            taken = found[:width]
            for high in range(1, REACH):
                taken = jnp.where(chunk == high, found[high * width : (high + 1) * width], taken)
            picked[pl.ds(pl.multiple_of(tap * width, width), width), :] = taken.astype(jnp.bfloat16)
            return 0

        lax.fori_loop(0, taps, one, 0, unroll=9 if taps % 9 == 0 else 1)

    def convolve(block):
        span = pl.ds(block * BLOCK, BLOCK)
        weight = conv[...].reshape(width, taps * width)
        pre_act = jnp.dot(weight, picked[...], preferred_element_type=jnp.float32)
        living = first_row + block * BLOCK + local < count
        hidden[:, span] = jnp.where(living, jnp.maximum(pre_act, 0.0), 0.0).astype(jnp.bfloat16)

    pick(0)
    take_chan(conv, conv_send, conv_recv)
    convolve(0)

    take_leaf(backward, back_send, back_recv)
    owner = dest[...] // group_count
    for part_index in range(chans):
        mine = owner[part_index : part_index + 1]

        def gain(source, held):
            return jnp.where(mine == source, backward[source].astype(jnp.float32), held)

        nothing = jnp.zeros((out_own, groups), jnp.float32)
        held = lax.fori_loop(0, leaves, gain, nothing, unroll=8)
        fetched_out[part_index] = held.astype(jnp.bfloat16)
    send_chan(lambda peer: fetched_out.at[peer], fetched, fetched_send, fetched_recv)
    fetched[chan] = fetched_out[chan]

    for block in range(1, quarter // BLOCK):
        pick(block)
        convolve(block)

    source_row = lax.broadcasted_iota(jnp.int32, (quarter, groups), 0)
    group_row = lax.broadcasted_iota(jnp.int32, (quarter, groups), 1) * KIDS
    for kid in range(KIDS):
        order = jnp.where(source_row == group_row + kid, 1.0, 0.0).astype(jnp.bfloat16)
        sorted_kid = jnp.dot(hidden[...], order, preferred_element_type=jnp.float32)
        stacked[pl.ds(kid * width, width), :] = sorted_kid.astype(jnp.bfloat16)

    take_chan(fetched, fetched_send, fetched_recv)
    part[...] = lax.dot_general(
        fetched[...].reshape(chans * out_own, groups), stacked[...],
        (((1,), (1,)), ((), ())), preferred_element_type=jnp.float32,
    ).reshape(part.shape)
    send_chan(lambda peer: part.at[peer], part_in, part_send, part_recv)

    take_chan(merge, merge_send, merge_recv)
    merged_out[...] = jnp.dot(
        merge[...].reshape(chans * out_own, KIDS * width), stacked[...],
        preferred_element_type=jnp.float32,
    ).astype(jnp.bfloat16).reshape(merged_out.shape)
    send_chan(lambda peer: merged_out.at[peer], merged, merged_send, merged_recv)
    merged[chan] = merged_out[chan]

    part_in[chan] = part[chan]
    take_chan(part_in, part_send, part_recv)
    term = part_in[0]
    for source in range(1, chans):
        term = term + part_in[source]
    across = KIDS * width // LANES
    for index in range(pieces):
        row, lane = index // across * PIECE_ROWS, index % across * LANES
        piece[index] = term[row : row + PIECE_ROWS, lane : lane + LANES]

    def piece_copy(turn):
        target = lax.rem(leaf + turn, pieces)
        return target, pltpu.make_async_remote_copy(
            src_ref=piece.at[target], dst_ref=piece_in.at[leaf], send_sem=piece_send.at[turn],
            recv_sem=piece_recv.at[leaf], device_id=(target, chan), device_id_type=MESH,
        )

    for turn in range(pieces):
        target, copy = piece_copy(turn)
        pl.when(target != leaf)(copy.start)

    take_chan(merged, merged_send, merged_recv)

    def fill_all(target, _):
        held = jnp.zeros((out_own, groups), jnp.float32)
        for source in range(chans):
            mine = owner[source : source + 1]
            held = held + jnp.where(mine == target, merged[source].astype(jnp.float32), 0.0)
        outbox[target] = held.astype(jnp.bfloat16)
        return 0

    lax.fori_loop(0, leaves, fill_all, 0, unroll=8)
    send_leaf(lambda peer: outbox.at[peer], inbox, box_send, box_recv)
    inbox[leaf] = outbox[leaf]

    @pl.when(leaf < pieces)
    def _():
        piece_in[leaf] = piece[leaf]
        take_leaf(piece_in, piece_send, piece_recv)

        def add(source, held):
            return held + piece_in[source]

        held = lax.fori_loop(1, leaves, add, piece_in[0], unroll=7 if leaves == 8 else 1)
        total[leaf] = held * (1.0 / math.sqrt(KIDS * group_count))
        each(leaves - 1, lambda turn: leaf_copy(
            lambda peer: total.at[leaf], total, total_send, total_recv, turn).start())

    take_leaf(inbox, box_send, box_recv)
    lane = lax.broadcasted_iota(jnp.int32, (1, LANES), 1) // pair_slots
    per_tile = LANES // pair_slots
    for tile in range(leaves // per_tile):
        whole = jnp.zeros((out_own, LANES), jnp.float32)
        for inside in range(per_tile):
            folded = inbox[tile * per_tile + inside].astype(jnp.float32)
            shift = pair_slots
            while shift < LANES:
                folded = folded + pltpu.roll(folded, shift, 1)
                shift *= 2
            whole = jnp.where(lane == inside, folded, whole)
        parents[:, pl.ds(tile * LANES, LANES)] = whole.astype(jnp.bfloat16)

    for index in range(pieces):
        arrival = pltpu.make_async_remote_copy(
            src_ref=total.at[index], dst_ref=total.at[index], send_sem=total_send.at[0],
            recv_sem=total_recv.at[index], device_id=(index, chan), device_id_type=MESH,
        )
        pl.when(leaf != index)(arrival.wait_recv)
    for index in range(pieces):
        row, lane_at = index // across * PIECE_ROWS, index % across * LANES
        grad[row : row + PIECE_ROWS, lane_at : lane_at + LANES] = total[index]

    pl.when(at_first & (leaf < leaves - 1))(from_left.wait_send)
    pl.when(at_last & (leaf > 0))(from_right.wait_send)
    for number, wait in sends:
        each(number, wait)
    for turn in range(pieces):
        target, copy = piece_copy(turn)
        pl.when(target != leaf)(copy.wait_send)

    @pl.when(leaf < pieces)
    def _():
        each(leaves - 1, lambda turn: leaf_copy(
            lambda peer: total.at[leaf], total, total_send, total_recv, turn).wait_send())


def per_device(features, neighbours, child_count, dest, conv_weight, merge_weight, parent_grad):
    width, row_count = features.shape
    taps = neighbours.shape[0]
    out_own = merge_weight.shape[2]
    group_count = row_count // KIDS
    leaves = lax.axis_size("leaf")
    chans = lax.axis_size("chan")
    pair_slots = group_count // leaves
    quarter = row_count // chans
    groups = quarter // KIDS
    repeats = groups // pair_slots
    pieces = min(leaves, out_own * KIDS * width // (PIECE_ROWS * LANES))
    conv_own = conv_weight.reshape(taps * width, -1).T
    merge_own = merge_weight.reshape(KIDS * width, -1).T
    blocks = parent_grad.reshape(out_own, leaves, 1, pair_slots)
    cotangent = jnp.broadcast_to(blocks, (out_own, leaves, repeats, pair_slots))
    cotangent = cotangent.reshape(out_own, leaves, groups).swapaxes(0, 1)

    anywhere = pl.BlockSpec(memory_space=pl.ANY)
    whole = pl.BlockSpec(memory_space=pltpu.VMEM)
    scalars = pl.BlockSpec(memory_space=pltpu.SMEM)
    bf16, f32 = jnp.bfloat16, jnp.float32

    def sems(*counts):
        return [pltpu.SemaphoreType.DMA((count,)) for count in counts]

    parents, grad = pl.pallas_call(
        functools.partial(octree_kernel, chans, leaves),
        out_shape=(
            jax.ShapeDtypeStruct((out_own, group_count), bf16),
            jax.ShapeDtypeStruct((out_own, KIDS * width), f32),
        ),
        in_specs=[anywhere, anywhere, scalars] + [whole] * 4,
        out_specs=(whole, whole),
        scratch_shapes=[
            pltpu.VMEM((width, quarter + 2 * HALO), bf16),
            pltpu.VMEM((taps, quarter), jnp.int32),
            pltpu.VMEM((chans, width // chans, taps * width), bf16),
            pltpu.VMEM((chans, out_own, KIDS * width), bf16),
            pltpu.VMEM((leaves, out_own, groups), bf16),
            pltpu.VMEM((chans, out_own, groups), bf16),
            pltpu.VMEM((chans, out_own, groups), bf16),
            pltpu.VMEM((taps * width, BLOCK), bf16),
            pltpu.VMEM((width, quarter), bf16),
            pltpu.VMEM((KIDS * width, groups), bf16),
            pltpu.VMEM((chans, out_own, groups), bf16),
            pltpu.VMEM((chans, out_own, groups), bf16),
            pltpu.VMEM((leaves, out_own, groups), bf16),
            pltpu.VMEM((leaves, out_own, groups), bf16),
            pltpu.VMEM((chans, out_own, KIDS * width), f32),
            pltpu.VMEM((chans, out_own, KIDS * width), f32),
            pltpu.VMEM((pieces, PIECE_ROWS, LANES), f32),
            pltpu.VMEM((leaves, PIECE_ROWS, LANES), f32),
            pltpu.VMEM((pieces, PIECE_ROWS, LANES), f32),
        ]
        + sems(4, 2, 2)
        + sems(chans, chans, chans, chans)
        + sems(leaves, leaves)
        + sems(chans, chans, chans, chans)
        + sems(leaves, leaves)
        + sems(chans, chans)
        + sems(pieces, leaves)
        + sems(leaves, leaves),
        compiler_params=pltpu.CompilerParams(
            collective_id=0, has_side_effects=True, vmem_limit_bytes=40 * 1024 * 1024
        ),
    )(
        features,
        neighbours,
        child_count,
        dest.reshape(chans, groups),
        conv_own,
        merge_own,
        cotangent,
    )
    return (parents, grad.T.reshape(KIDS, width, out_own))


def solution(mesh):
    in_specs = (
        P(None, "leaf"),
        P(None, "leaf"),
        P("leaf"),
        P("leaf"),
        P(None, None, "chan"),
        P(None, None, "chan"),
        P("chan", "leaf"),
    )
    out_specs = (P("chan", "leaf"), P(None, None, "chan"))
    return jax.shard_map(
        per_device, mesh=mesh, in_specs=in_specs, out_specs=out_specs, check_vma=False
    )
```

```python
import functools
import math

import jax
import jax.numpy as jnp
from jax import lax
from jax.experimental import pallas as pl
from jax.experimental.pallas import tpu as pltpu
from jax.sharding import PartitionSpec as P

KIDS = 8
HALO = 1024
LO = 256
BLOCK = 256
REACH = (2 * HALO + BLOCK) // LO
LANES = 128
PIECE_ROWS = 16
MESH = pl.DeviceIdType.MESH


def each(count, step):
    if count <= 8:
        for turn in range(count):
            step(turn)
    else:
        lax.fori_loop(0, count, lambda turn, _: (step(turn), 0)[1], 0)


def octree_kernel(
    chans,
    leaves,
    features,
    neighbours,
    child_count,
    dest,
    conv_own,
    merge_own,
    cotangent_own,
    parents,
    grad,
    window,
    offsets,
    conv,
    merge,
    cotangent,
    backward,
    fetched_out,
    fetched,
    picked,
    stacked,
    merged_out,
    merged,
    outbox,
    inbox,
    part,
    part_out,
    part_in,
    piece,
    piece_in,
    total,
    local_sem,
    halo_send,
    halo_recv,
    conv_send,
    conv_recv,
    merge_send,
    merge_recv,
    back_send,
    back_recv,
    fetched_send,
    fetched_recv,
    merged_send,
    merged_recv,
    box_send,
    box_recv,
    part_send,
    part_recv,
    piece_send,
    piece_recv,
    total_send,
    total_recv,
):
    leaf = lax.axis_index("leaf")
    chan = lax.axis_index("chan")
    width, row_count = features.shape
    taps = neighbours.shape[0]
    quarter = row_count // chans
    groups = quarter // KIDS
    group_count = row_count // KIDS
    pair_slots = group_count // leaves
    out_own = merge_own.shape[1]
    pieces = piece.shape[0]
    first_row = pl.multiple_of(chan * quarter, LO)

    def chan_copy(src, dst, send, recv, turn):
        peer = lax.rem(chan + turn + 1, chans)
        return pltpu.make_async_remote_copy(
            src_ref=src(peer), dst_ref=dst.at[chan], send_sem=send.at[turn],
            recv_sem=recv.at[chan], device_id=(leaf, peer), device_id_type=MESH,
        )

    def chan_arrival(dst, send, recv, turn):
        peer = lax.rem(chan + turn + 1, chans)
        return pltpu.make_async_remote_copy(
            src_ref=dst.at[peer], dst_ref=dst.at[peer], send_sem=send.at[turn],
            recv_sem=recv.at[peer], device_id=(leaf, peer), device_id_type=MESH,
        )

    def leaf_copy(src, dst, send, recv, turn):
        peer = lax.rem(leaf + turn + 1, leaves)
        return pltpu.make_async_remote_copy(
            src_ref=src(peer), dst_ref=dst.at[leaf], send_sem=send.at[turn],
            recv_sem=recv.at[leaf], device_id=(peer, chan), device_id_type=MESH,
        )

    def leaf_arrival(dst, send, recv, turn):
        peer = lax.rem(leaf + turn + 1, leaves)
        return pltpu.make_async_remote_copy(
            src_ref=dst.at[peer], dst_ref=dst.at[peer], send_sem=send.at[turn],
            recv_sem=recv.at[peer], device_id=(peer, chan), device_id_type=MESH,
        )

    def near(at, size):
        return features.at[:, pl.ds(at, size)]

    left_local = pltpu.make_async_copy(
        near(pl.multiple_of(jnp.maximum(first_row - HALO, 0), LO), HALO),
        window.at[:, pl.ds(0, HALO)], local_sem.at[0],
    )
    right_local = pltpu.make_async_copy(
        near(pl.multiple_of(jnp.minimum(first_row + quarter, row_count - HALO), LO), HALO),
        window.at[:, pl.ds(HALO + quarter, HALO)], local_sem.at[1],
    )
    centre_local = pltpu.make_async_copy(
        near(first_row, quarter), window.at[:, pl.ds(HALO, quarter)], local_sem.at[2]
    )
    offsets_local = pltpu.make_async_copy(
        neighbours.at[:, pl.ds(first_row, quarter)], offsets, local_sem.at[3]
    )
    from_left = pltpu.make_async_remote_copy(
        src_ref=near(row_count - HALO, HALO), dst_ref=window.at[:, pl.ds(0, HALO)],
        send_sem=halo_send.at[0], recv_sem=halo_recv.at[0],
        device_id=(jnp.minimum(leaf + 1, leaves - 1), chan), device_id_type=MESH,
    )
    from_right = pltpu.make_async_remote_copy(
        src_ref=near(0, HALO), dst_ref=window.at[:, pl.ds(HALO + quarter, HALO)],
        send_sem=halo_send.at[1], recv_sem=halo_recv.at[1],
        device_id=(jnp.maximum(leaf - 1, 0), chan), device_id_type=MESH,
    )
    at_first = chan == 0
    at_last = chan == chans - 1

    offsets_local.start()
    centre_local.start()
    pl.when(jnp.logical_not(at_first))(left_local.start)
    pl.when(jnp.logical_not(at_last))(right_local.start)

    barrier = pltpu.get_barrier_semaphore()

    def greet_chan(turn):
        peer = lax.rem(chan + turn + 1, chans)
        pl.semaphore_signal(barrier, inc=1, device_id=(leaf, peer), device_id_type=MESH)

    def greet_leaf(turn):
        peer = lax.rem(leaf + turn + 1, leaves)
        pl.semaphore_signal(barrier, inc=1, device_id=(peer, chan), device_id_type=MESH)

    each(chans - 1, greet_chan)
    each(leaves - 1, greet_leaf)

    for tap in range(0, taps, 2):
        beside = jnp.concatenate([conv_own[at] for at in range(tap, min(tap + 2, taps))], axis=1)
        conv[chan, :, tap * width : tap * width + beside.shape[1]] = beside
    for kid in range(0, KIDS, 2):
        beside = jnp.concatenate([merge_own[kid], merge_own[kid + 1]], axis=1)
        merge[chan, :, kid * width : (kid + 2) * width] = beside
    lane = lax.broadcasted_iota(jnp.int32, (1, LANES), 1) // pair_slots
    per_tile = LANES // pair_slots
    for tile in range(leaves // per_tile):
        held = cotangent_own[:, tile * LANES : (tile + 1) * LANES].astype(jnp.float32)
        for inside in range(per_tile):
            spread = jnp.where(lane == inside, held, 0.0)
            shift = pair_slots
            while shift < LANES:
                spread = spread + pltpu.roll(spread, shift, 1)
                shift *= 2
            cotangent[tile * per_tile + inside] = spread.astype(jnp.bfloat16)

    pl.semaphore_wait(barrier, chans + leaves - 2)

    pl.when(at_first & (leaf < leaves - 1))(from_left.start)
    pl.when(at_last & (leaf > 0))(from_right.start)
    sends = []

    def send_chan(src, dst, send, recv):
        each(chans - 1, lambda turn: chan_copy(src, dst, send, recv, turn).start())
        sends.append((chans - 1, lambda turn: chan_copy(src, dst, send, recv, turn).wait_send()))

    def send_leaf(src, dst, send, recv):
        each(leaves - 1, lambda turn: leaf_copy(src, dst, send, recv, turn).start())
        sends.append((leaves - 1, lambda turn: leaf_copy(src, dst, send, recv, turn).wait_send()))

    def take_chan(dst, send, recv):
        each(chans - 1, lambda turn: chan_arrival(dst, send, recv, turn).wait_recv())

    def take_leaf(dst, send, recv):
        each(leaves - 1, lambda turn: leaf_arrival(dst, send, recv, turn).wait_recv())

    send_chan(lambda peer: conv.at[chan], conv, conv_send, conv_recv)
    send_leaf(lambda peer: cotangent.at[peer], backward, back_send, back_recv)
    send_chan(lambda peer: merge.at[chan], merge, merge_send, merge_recv)
    backward[leaf] = cotangent[leaf]

    @pl.when(at_first & (leaf == 0))
    def _():
        window[:, :HALO] = jnp.zeros((width, HALO), jnp.bfloat16)

    @pl.when(at_last & (leaf == leaves - 1))
    def _():
        window[:, HALO + quarter :] = jnp.zeros((width, HALO), jnp.bfloat16)

    offsets_local.wait()
    centre_local.wait()
    pl.when(jnp.logical_not(at_first))(left_local.wait)
    pl.when(jnp.logical_not(at_last))(right_local.wait)

    slot = lax.broadcasted_iota(jnp.int32, (LO, BLOCK), 0).astype(jnp.float32).astype(jnp.bfloat16)
    local = lax.broadcasted_iota(jnp.int32, (1, BLOCK), 1)
    count = child_count[0]

    blocks = quarter // BLOCK
    flip = jnp.where(at_first, 1, 0)

    def block_of(turn):
        return jnp.where(at_first, blocks - 1 - turn, turn)

    def span_of(block):
        return pl.ds(pl.multiple_of(block * BLOCK, BLOCK), BLOCK)

    def chunk_at(number):
        return window[:, pl.ds(pl.multiple_of(number * LO, LO), LO)]

    def over_taps(step):
        lax.fori_loop(0, taps, lambda tap, _: (step(tap), 0)[1], 0, unroll=9 if taps % 9 == 0 else 1)

    def split(tap, block):
        offset = offsets[pl.ds(tap, 1), span_of(block)]
        place = local + offset
        chunk = place // LO
        inner = jnp.where(offset >= 0, place - chunk * LO, -1)
        inner = inner.astype(jnp.float32).astype(jnp.bfloat16)
        return chunk, jnp.where(slot == inner, jnp.bfloat16(1), jnp.bfloat16(0))

    def tap_rows(tap):
        return pl.ds(pl.multiple_of(tap * width, width), width)

    def pick(block):
        source = jnp.concatenate([chunk_at(block + high) for high in range(REACH)], axis=0)

        def one(tap):
            chunk, hot = split(tap, block)
            found = jnp.dot(source, hot, preferred_element_type=jnp.float32)
            taken = found[:width]
            for high in range(1, REACH):
                taken = jnp.where(chunk == high, found[high * width : (high + 1) * width], taken)
            picked[tap_rows(tap), :] = taken.astype(jnp.bfloat16)

        over_taps(one)

    def pick_local(block):
        first = block + flip
        source = jnp.concatenate([chunk_at(first + high) for high in range(REACH - 1)], axis=0)

        def one(tap):
            chunk, hot = split(tap, block)
            found = jnp.dot(source, hot, preferred_element_type=jnp.float32)
            taken = jnp.zeros((width, BLOCK), jnp.float32)
            for high in range(REACH - 1):
                here = chunk == high + flip
                taken = jnp.where(here, found[high * width : (high + 1) * width], taken)
            picked[tap_rows(tap), :] = taken.astype(jnp.bfloat16)

        over_taps(one)

    def pick_halo(block):
        far = (REACH - 1) * (1 - flip)
        source = chunk_at(block + far)

        def one(tap):
            chunk, hot = split(tap, block)
            found = jnp.dot(source, hot, preferred_element_type=jnp.float32)
            held = picked[tap_rows(tap), :].astype(jnp.float32)
            picked[tap_rows(tap), :] = jnp.where(chunk == far, found, held).astype(jnp.bfloat16)

        over_taps(one)

    def convolve(block, fresh):
        weight = conv[...].reshape(width, taps * width)
        pre_act = jnp.dot(weight, picked[...], preferred_element_type=jnp.float32)
        living = first_row + block * BLOCK + local < count
        hidden = jnp.where(living, jnp.maximum(pre_act, 0.0), 0.0).astype(jnp.bfloat16)
        kids = BLOCK // groups
        for kid in range(0, KIDS, kids):
            wanted = lax.broadcasted_iota(jnp.int32, (1, BLOCK), 1)
            wanted = wanted % groups * KIDS + kid + wanted // groups - block * BLOCK
            wanted = jnp.where((wanted >= 0) & (wanted < BLOCK), wanted, -1)
            wanted = wanted.astype(jnp.float32).astype(jnp.bfloat16)
            order = jnp.where(slot == wanted, jnp.bfloat16(1), jnp.bfloat16(0))
            moved = jnp.dot(hidden, order, preferred_element_type=jnp.float32).astype(jnp.bfloat16)
            for inside in range(kids):
                rows = pl.ds((kid + inside) * width, width)
                new = moved[:, inside * groups : (inside + 1) * groups]
                stacked[rows, :] = new if fresh else stacked[rows, :] + new

    pick_local(block_of(0))
    pl.when(at_first & (leaf > 0))(from_left.wait_recv)
    pl.when(at_last & (leaf < leaves - 1))(from_right.wait_recv)
    pick_halo(block_of(0))
    take_chan(conv, conv_send, conv_recv)
    convolve(block_of(0), True)

    take_leaf(backward, back_send, back_recv)
    owner = dest[...] // group_count
    for part_index in range(chans):
        mine = owner[part_index : part_index + 1]

        def gain(source, held):
            return jnp.where(mine == source, backward[source].astype(jnp.float32), held)

        nothing = jnp.zeros((out_own, groups), jnp.float32)
        held = lax.fori_loop(0, leaves, gain, nothing, unroll=8)
        fetched_out[part_index] = held.astype(jnp.bfloat16)
    send_chan(lambda peer: fetched_out.at[peer], fetched, fetched_send, fetched_recv)
    fetched[chan] = fetched_out[chan]

    for turn in range(1, blocks):
        pick(block_of(turn))
        convolve(block_of(turn), False)

    take_chan(fetched, fetched_send, fetched_recv)
    part[...] = lax.dot_general(
        fetched[...].reshape(chans * out_own, groups), stacked[...],
        (((1,), (1,)), ((), ())), preferred_element_type=jnp.float32,
    ).reshape(part.shape)
    part_out[...] = part[...].astype(jnp.bfloat16)
    send_chan(lambda peer: part_out.at[peer], part_in, part_send, part_recv)

    take_chan(merge, merge_send, merge_recv)
    merged_out[...] = jnp.dot(
        merge[...].reshape(chans * out_own, KIDS * width), stacked[...],
        preferred_element_type=jnp.float32,
    ).astype(jnp.bfloat16).reshape(merged_out.shape)
    send_chan(lambda peer: merged_out.at[peer], merged, merged_send, merged_recv)
    merged[chan] = merged_out[chan]

    take_chan(part_in, part_send, part_recv)
    term = part[chan]
    for turn in range(1, chans):
        term = term + part_in[lax.rem(chan + turn, chans)].astype(jnp.float32)
    across = KIDS * width // LANES
    for index in range(pieces):
        row, column = index // across * PIECE_ROWS, index % across * LANES
        piece[index] = term[row : row + PIECE_ROWS, column : column + LANES]

    def piece_copy(turn):
        target = lax.rem(leaf + turn, pieces)
        return target, pltpu.make_async_remote_copy(
            src_ref=piece.at[target], dst_ref=piece_in.at[leaf], send_sem=piece_send.at[turn],
            recv_sem=piece_recv.at[leaf], device_id=(target, chan), device_id_type=MESH,
        )

    for turn in range(pieces):
        target, copy = piece_copy(turn)
        pl.when(target != leaf)(copy.start)

    take_chan(merged, merged_send, merged_recv)

    def fill_all(target, _):
        held = jnp.zeros((out_own, groups), jnp.float32)
        for source in range(chans):
            mine = owner[source : source + 1]
            held = held + jnp.where(mine == target, merged[source].astype(jnp.float32), 0.0)
        outbox[target] = held.astype(jnp.bfloat16)
        return 0

    lax.fori_loop(0, leaves, fill_all, 0, unroll=8)
    send_leaf(lambda peer: outbox.at[peer], inbox, box_send, box_recv)
    inbox[leaf] = outbox[leaf]

    @pl.when(leaf < pieces)
    def _():
        piece_in[leaf] = piece[leaf]
        take_leaf(piece_in, piece_send, piece_recv)

        def add(source, held):
            return held + piece_in[source]

        held = lax.fori_loop(1, leaves, add, piece_in[0], unroll=7 if leaves == 8 else 1)
        total[leaf] = held * (1.0 / math.sqrt(KIDS * group_count))
        each(leaves - 1, lambda turn: leaf_copy(
            lambda peer: total.at[leaf], total, total_send, total_recv, turn).start())

    take_leaf(inbox, box_send, box_recv)
    for tile in range(leaves // per_tile):
        whole = jnp.zeros((out_own, LANES), jnp.float32)
        for inside in range(per_tile):
            folded = inbox[tile * per_tile + inside].astype(jnp.float32)
            shift = pair_slots
            while shift < LANES:
                folded = folded + pltpu.roll(folded, shift, 1)
                shift *= 2
            whole = jnp.where(lane == inside, folded, whole)
        parents[:, pl.ds(tile * LANES, LANES)] = whole.astype(jnp.bfloat16)

    for index in range(pieces):
        arrival = pltpu.make_async_remote_copy(
            src_ref=total.at[index], dst_ref=total.at[index], send_sem=total_send.at[0],
            recv_sem=total_recv.at[index], device_id=(index, chan), device_id_type=MESH,
        )
        pl.when(leaf != index)(arrival.wait_recv)
    for index in range(pieces):
        row, kid = index // across * PIECE_ROWS, index % across * (LANES // width)
        summed = total[index]
        for inside in range(LANES // width):
            one_kid = summed[:, inside * width : (inside + 1) * width]
            grad[kid + inside, row : row + PIECE_ROWS, :] = one_kid

    pl.when(at_first & (leaf < leaves - 1))(from_left.wait_send)
    pl.when(at_last & (leaf > 0))(from_right.wait_send)
    for number, wait in sends:
        each(number, wait)
    for turn in range(pieces):
        target, copy = piece_copy(turn)
        pl.when(target != leaf)(copy.wait_send)

    @pl.when(leaf < pieces)
    def _():
        each(leaves - 1, lambda turn: leaf_copy(
            lambda peer: total.at[leaf], total, total_send, total_recv, turn).wait_send())


def per_device(features, neighbours, child_count, dest, conv_weight, merge_weight, parent_grad):
    width, row_count = features.shape
    taps = neighbours.shape[0]
    out_own = merge_weight.shape[2]
    group_count = row_count // KIDS
    leaves = lax.axis_size("leaf")
    chans = lax.axis_size("chan")
    quarter = row_count // chans
    groups = quarter // KIDS
    pieces = min(leaves, out_own * KIDS * width // (PIECE_ROWS * LANES))
    anywhere = pl.BlockSpec(memory_space=pl.ANY)
    whole = pl.BlockSpec(memory_space=pltpu.VMEM)
    scalars = pl.BlockSpec(memory_space=pltpu.SMEM)
    bf16, f32 = jnp.bfloat16, jnp.float32

    def sems(*counts):
        return [pltpu.SemaphoreType.DMA((count,)) for count in counts]

    parents, grad = pl.pallas_call(
        functools.partial(octree_kernel, chans, leaves),
        out_shape=(
            jax.ShapeDtypeStruct((out_own, group_count), bf16),
            jax.ShapeDtypeStruct((KIDS, out_own, width), f32),
        ),
        in_specs=[anywhere, anywhere, scalars] + [whole] * 4,
        out_specs=(whole, whole),
        scratch_shapes=[
            pltpu.VMEM((width, quarter + 2 * HALO), bf16),
            pltpu.VMEM((taps, quarter), jnp.int32),
            pltpu.VMEM((chans, width // chans, taps * width), bf16),
            pltpu.VMEM((chans, out_own, KIDS * width), bf16),
            pltpu.VMEM((leaves, out_own, groups), bf16),
            pltpu.VMEM((leaves, out_own, groups), bf16),
            pltpu.VMEM((chans, out_own, groups), bf16),
            pltpu.VMEM((chans, out_own, groups), bf16),
            pltpu.VMEM((taps * width, BLOCK), bf16),
            pltpu.VMEM((KIDS * width, groups), bf16),
            pltpu.VMEM((chans, out_own, groups), bf16),
            pltpu.VMEM((chans, out_own, groups), bf16),
            pltpu.VMEM((leaves, out_own, groups), bf16),
            pltpu.VMEM((leaves, out_own, groups), bf16),
            pltpu.VMEM((chans, out_own, KIDS * width), f32),
            pltpu.VMEM((chans, out_own, KIDS * width), bf16),
            pltpu.VMEM((chans, out_own, KIDS * width), bf16),
            pltpu.VMEM((pieces, PIECE_ROWS, LANES), f32),
            pltpu.VMEM((leaves, PIECE_ROWS, LANES), f32),
            pltpu.VMEM((pieces, PIECE_ROWS, LANES), f32),
        ]
        + sems(4, 2, 2)
        + sems(chans, chans, chans, chans)
        + sems(leaves, leaves)
        + sems(chans, chans, chans, chans)
        + sems(leaves, leaves)
        + sems(chans, chans)
        + sems(pieces, leaves)
        + sems(leaves, leaves),
        compiler_params=pltpu.CompilerParams(
            collective_id=0, has_side_effects=True, vmem_limit_bytes=56 * 1024 * 1024
        ),
    )(
        features,
        neighbours,
        child_count,
        dest.reshape(chans, groups),
        conv_weight.swapaxes(1, 2),
        merge_weight.swapaxes(1, 2),
        parent_grad,
    )
    return (parents, grad.swapaxes(1, 2))


def solution(mesh):
    in_specs = (
        P(None, "leaf"),
        P(None, "leaf"),
        P("leaf"),
        P("leaf"),
        P(None, None, "chan"),
        P(None, None, "chan"),
        P("chan", "leaf"),
    )
    out_specs = (P("chan", "leaf"), P(None, None, "chan"))
    return jax.shard_map(
        per_device, mesh=mesh, in_specs=in_specs, out_specs=out_specs, check_vma=False
    )
```

```python
import functools
import math

import jax
import jax.numpy as jnp
from jax import lax
from jax.experimental import pallas as pl
from jax.experimental.pallas import tpu as pltpu
from jax.sharding import PartitionSpec as P

KIDS = 8
HALO = 1024
LO = 256
BLOCK = 256
REACH = (2 * HALO + BLOCK) // LO
LANES = 128
PIECE_ROWS = 16
MESH = pl.DeviceIdType.MESH


def each(count, step):
    if count <= 8:
        for turn in range(count):
            step(turn)
    else:
        lax.fori_loop(0, count, lambda turn, _: (step(turn), 0)[1], 0)


def octree_kernel(
    chans,
    leaves,
    features,
    neighbours,
    child_count,
    dest,
    conv_own,
    merge_own,
    cotangent_own,
    parents,
    grad,
    window,
    offsets,
    conv,
    merge,
    cotangent,
    backward,
    fetched_out,
    fetched,
    picked,
    stacked,
    merged_out,
    merged,
    outbox,
    inbox,
    part,
    part_out,
    part_in,
    piece,
    piece_in,
    total,
    local_sem,
    halo_send,
    halo_recv,
    conv_send,
    conv_recv,
    merge_send,
    merge_recv,
    back_send,
    back_recv,
    fetched_send,
    fetched_recv,
    merged_send,
    merged_recv,
    box_send,
    box_recv,
    part_send,
    part_recv,
    piece_send,
    piece_recv,
    total_send,
    total_recv,
):
    leaf = lax.axis_index("leaf")
    chan = lax.axis_index("chan")
    width, row_count = features.shape
    taps = neighbours.shape[0]
    quarter = row_count // chans
    groups = quarter // KIDS
    group_count = row_count // KIDS
    pair_slots = group_count // leaves
    out_own = merge_own.shape[1]
    pieces = piece.shape[0]
    first_row = pl.multiple_of(chan * quarter, LO)

    def chan_copy(src, dst, send, recv, turn):
        peer = lax.rem(chan + turn + 1, chans)
        return pltpu.make_async_remote_copy(
            src_ref=src(peer), dst_ref=dst.at[chan], send_sem=send.at[turn],
            recv_sem=recv.at[chan], device_id=(leaf, peer), device_id_type=MESH,
        )

    def chan_arrival(dst, send, recv, turn):
        peer = lax.rem(chan + turn + 1, chans)
        return pltpu.make_async_remote_copy(
            src_ref=dst.at[peer], dst_ref=dst.at[peer], send_sem=send.at[turn],
            recv_sem=recv.at[peer], device_id=(leaf, peer), device_id_type=MESH,
        )

    def leaf_copy(src, dst, send, recv, turn):
        peer = lax.rem(leaf + turn + 1, leaves)
        return pltpu.make_async_remote_copy(
            src_ref=src(peer), dst_ref=dst.at[leaf], send_sem=send.at[turn],
            recv_sem=recv.at[leaf], device_id=(peer, chan), device_id_type=MESH,
        )

    def leaf_arrival(dst, send, recv, turn):
        peer = lax.rem(leaf + turn + 1, leaves)
        return pltpu.make_async_remote_copy(
            src_ref=dst.at[peer], dst_ref=dst.at[peer], send_sem=send.at[turn],
            recv_sem=recv.at[peer], device_id=(peer, chan), device_id_type=MESH,
        )

    def near(at, size):
        return features.at[:, pl.ds(at, size)]

    left_local = pltpu.make_async_copy(
        near(pl.multiple_of(jnp.maximum(first_row - HALO, 0), LO), HALO),
        window.at[:, pl.ds(0, HALO)], local_sem.at[0],
    )
    right_local = pltpu.make_async_copy(
        near(pl.multiple_of(jnp.minimum(first_row + quarter, row_count - HALO), LO), HALO),
        window.at[:, pl.ds(HALO + quarter, HALO)], local_sem.at[1],
    )
    centre_local = pltpu.make_async_copy(
        near(first_row, quarter), window.at[:, pl.ds(HALO, quarter)], local_sem.at[2]
    )
    offsets_local = pltpu.make_async_copy(
        neighbours.at[:, pl.ds(first_row, quarter)], offsets, local_sem.at[3]
    )
    from_left = pltpu.make_async_remote_copy(
        src_ref=near(row_count - HALO, HALO), dst_ref=window.at[:, pl.ds(0, HALO)],
        send_sem=halo_send.at[0], recv_sem=halo_recv.at[0],
        device_id=(jnp.minimum(leaf + 1, leaves - 1), chan), device_id_type=MESH,
    )
    from_right = pltpu.make_async_remote_copy(
        src_ref=near(0, HALO), dst_ref=window.at[:, pl.ds(HALO + quarter, HALO)],
        send_sem=halo_send.at[1], recv_sem=halo_recv.at[1],
        device_id=(jnp.maximum(leaf - 1, 0), chan), device_id_type=MESH,
    )
    at_first = chan == 0
    at_last = chan == chans - 1

    offsets_local.start()
    centre_local.start()
    pl.when(jnp.logical_not(at_first))(left_local.start)
    pl.when(jnp.logical_not(at_last))(right_local.start)

    barrier = pltpu.get_barrier_semaphore()

    def greet_chan(turn):
        peer = lax.rem(chan + turn + 1, chans)
        pl.semaphore_signal(barrier, inc=1, device_id=(leaf, peer), device_id_type=MESH)

    def greet_leaf(turn):
        peer = lax.rem(leaf + turn + 1, leaves)
        pl.semaphore_signal(barrier, inc=1, device_id=(peer, chan), device_id_type=MESH)

    each(chans - 1, greet_chan)
    each(leaves - 1, greet_leaf)

    for tap in range(0, taps, 2):
        beside = jnp.concatenate([conv_own[at] for at in range(tap, min(tap + 2, taps))], axis=1)
        conv[chan, :, tap * width : tap * width + beside.shape[1]] = beside
    for kid in range(0, KIDS, 2):
        beside = jnp.concatenate([merge_own[kid], merge_own[kid + 1]], axis=1)
        merge[chan, :, kid * width : (kid + 2) * width] = beside
    lane = lax.broadcasted_iota(jnp.int32, (1, LANES), 1) // pair_slots
    per_tile = LANES // pair_slots
    for tile in range(leaves // per_tile):
        held = cotangent_own[:, tile * LANES : (tile + 1) * LANES].astype(jnp.float32)
        for inside in range(per_tile):
            spread = jnp.where(lane == inside, held, 0.0)
            shift = pair_slots
            while shift < LANES:
                spread = spread + pltpu.roll(spread, shift, 1)
                shift *= 2
            cotangent[tile * per_tile + inside] = spread.astype(jnp.bfloat16)

    pl.semaphore_wait(barrier, chans + leaves - 2)

    pl.when(at_first & (leaf < leaves - 1))(from_left.start)
    pl.when(at_last & (leaf > 0))(from_right.start)
    sends = []

    def send_chan(src, dst, send, recv):
        each(chans - 1, lambda turn: chan_copy(src, dst, send, recv, turn).start())
        sends.append((chans - 1, lambda turn: chan_copy(src, dst, send, recv, turn).wait_send()))

    def send_leaf(src, dst, send, recv):
        each(leaves - 1, lambda turn: leaf_copy(src, dst, send, recv, turn).start())
        sends.append((leaves - 1, lambda turn: leaf_copy(src, dst, send, recv, turn).wait_send()))

    def take_chan(dst, send, recv):
        each(chans - 1, lambda turn: chan_arrival(dst, send, recv, turn).wait_recv())

    def take_leaf(dst, send, recv):
        each(leaves - 1, lambda turn: leaf_arrival(dst, send, recv, turn).wait_recv())

    send_chan(lambda peer: conv.at[chan], conv, conv_send, conv_recv)
    send_leaf(lambda peer: cotangent.at[peer], backward, back_send, back_recv)
    send_chan(lambda peer: merge.at[chan], merge, merge_send, merge_recv)
    backward[leaf] = cotangent[leaf]

    @pl.when(at_first & (leaf == 0))
    def _():
        window[:, :HALO] = jnp.zeros((width, HALO), jnp.bfloat16)

    @pl.when(at_last & (leaf == leaves - 1))
    def _():
        window[:, HALO + quarter :] = jnp.zeros((width, HALO), jnp.bfloat16)

    offsets_local.wait()
    centre_local.wait()
    pl.when(jnp.logical_not(at_first))(left_local.wait)
    pl.when(jnp.logical_not(at_last))(right_local.wait)

    slot = lax.broadcasted_iota(jnp.int32, (LO, BLOCK), 0).astype(jnp.float32).astype(jnp.bfloat16)
    local = lax.broadcasted_iota(jnp.int32, (1, BLOCK), 1)
    count = child_count[0]

    blocks = quarter // BLOCK
    centre = taps // 2
    flip = jnp.where(at_first, 1, 0)

    def block_of(turn):
        return jnp.where(at_first, blocks - 1 - turn, turn)

    def span_of(block):
        return pl.ds(pl.multiple_of(block * BLOCK, BLOCK), BLOCK)

    def chunk_at(number):
        return window[:, pl.ds(pl.multiple_of(number * LO, LO), LO)]

    def over_taps(step):
        for low, high in ((0, centre), (centre + 1, taps)):
            lax.fori_loop(low, high, lambda tap, _: (step(tap), 0)[1], 0, unroll=high - low)

    def split(tap, block):
        offset = offsets[pl.ds(tap, 1), span_of(block)]
        place = local + offset
        chunk = place // LO
        inner = jnp.where(offset >= 0, place - chunk * LO, -1)
        inner = inner.astype(jnp.float32).astype(jnp.bfloat16)
        return chunk, jnp.where(slot == inner, jnp.bfloat16(1), jnp.bfloat16(0))

    def tap_rows(tap):
        return pl.ds(pl.multiple_of(tap * width, width), width)

    def own_rows(block):
        picked[pl.ds(centre * width, width), :] = chunk_at(block + HALO // LO)

    def pick(block):
        own_rows(block)
        source = jnp.concatenate([chunk_at(block + high) for high in range(REACH)], axis=0)

        def one(tap):
            chunk, hot = split(tap, block)
            found = jnp.dot(source, hot, preferred_element_type=jnp.float32)
            taken = found[:width]
            for high in range(1, REACH):
                taken = jnp.where(chunk == high, found[high * width : (high + 1) * width], taken)
            picked[tap_rows(tap), :] = taken.astype(jnp.bfloat16)

        over_taps(one)

    def pick_local(block):
        first = block + flip
        own_rows(block)
        source = jnp.concatenate([chunk_at(first + high) for high in range(REACH - 1)], axis=0)

        def one(tap):
            chunk, hot = split(tap, block)
            found = jnp.dot(source, hot, preferred_element_type=jnp.float32)
            taken = jnp.zeros((width, BLOCK), jnp.float32)
            for high in range(REACH - 1):
                here = chunk == high + flip
                taken = jnp.where(here, found[high * width : (high + 1) * width], taken)
            picked[tap_rows(tap), :] = taken.astype(jnp.bfloat16)

        over_taps(one)

    def pick_halo(block):
        far = (REACH - 1) * (1 - flip)
        source = chunk_at(block + far)

        def one(tap):
            chunk, hot = split(tap, block)
            found = jnp.dot(source, hot, preferred_element_type=jnp.float32)
            held = picked[tap_rows(tap), :].astype(jnp.float32)
            picked[tap_rows(tap), :] = jnp.where(chunk == far, found, held).astype(jnp.bfloat16)

        over_taps(one)

    def convolve(block, fresh):
        weight = conv[...].reshape(width, taps * width)
        pre_act = jnp.dot(weight, picked[...], preferred_element_type=jnp.float32)
        living = first_row + block * BLOCK + local < count
        hidden = jnp.where(living, jnp.maximum(pre_act, 0.0), 0.0).astype(jnp.bfloat16)
        kids = BLOCK // groups
        for kid in range(0, KIDS, kids):
            wanted = lax.broadcasted_iota(jnp.int32, (1, BLOCK), 1)
            wanted = wanted % groups * KIDS + kid + wanted // groups - block * BLOCK
            wanted = jnp.where((wanted >= 0) & (wanted < BLOCK), wanted, -1)
            wanted = wanted.astype(jnp.float32).astype(jnp.bfloat16)
            order = jnp.where(slot == wanted, jnp.bfloat16(1), jnp.bfloat16(0))
            moved = jnp.dot(hidden, order, preferred_element_type=jnp.float32).astype(jnp.bfloat16)
            for inside in range(kids):
                rows = pl.ds((kid + inside) * width, width)
                new = moved[:, inside * groups : (inside + 1) * groups]
                stacked[rows, :] = new if fresh else stacked[rows, :] + new

    pick_local(block_of(0))
    pl.when(at_first & (leaf > 0))(from_left.wait_recv)
    pl.when(at_last & (leaf < leaves - 1))(from_right.wait_recv)
    pick_halo(block_of(0))
    take_chan(conv, conv_send, conv_recv)
    convolve(block_of(0), True)

    take_leaf(backward, back_send, back_recv)
    owner = dest[...] // group_count
    for part_index in range(chans):
        mine = owner[part_index : part_index + 1]

        def gain(source, held):
            return jnp.where(mine == source, backward[source].astype(jnp.float32), held)

        nothing = jnp.zeros((out_own, groups), jnp.float32)
        held = lax.fori_loop(0, leaves, gain, nothing, unroll=8)
        fetched_out[part_index] = held.astype(jnp.bfloat16)
    send_chan(lambda peer: fetched_out.at[peer], fetched, fetched_send, fetched_recv)
    fetched[chan] = fetched_out[chan]

    for turn in range(1, blocks):
        pick(block_of(turn))
        convolve(block_of(turn), False)

    take_chan(fetched, fetched_send, fetched_recv)
    part[...] = lax.dot_general(
        fetched[...].reshape(chans * out_own, groups), stacked[...],
        (((1,), (1,)), ((), ())), preferred_element_type=jnp.float32,
    ).reshape(part.shape)
    part_out[...] = part[...].astype(jnp.bfloat16)
    send_chan(lambda peer: part_out.at[peer], part_in, part_send, part_recv)

    take_chan(merge, merge_send, merge_recv)
    merged_out[...] = jnp.dot(
        merge[...].reshape(chans * out_own, KIDS * width), stacked[...],
        preferred_element_type=jnp.float32,
    ).astype(jnp.bfloat16).reshape(merged_out.shape)
    send_chan(lambda peer: merged_out.at[peer], merged, merged_send, merged_recv)
    merged[chan] = merged_out[chan]

    take_chan(part_in, part_send, part_recv)
    term = part[chan]
    for turn in range(1, chans):
        term = term + part_in[lax.rem(chan + turn, chans)].astype(jnp.float32)
    across = KIDS * width // LANES
    for index in range(pieces):
        row, column = index // across * PIECE_ROWS, index % across * LANES
        piece[index] = term[row : row + PIECE_ROWS, column : column + LANES]

    def piece_copy(turn):
        target = lax.rem(leaf + turn, pieces)
        return target, pltpu.make_async_remote_copy(
            src_ref=piece.at[target], dst_ref=piece_in.at[leaf], send_sem=piece_send.at[turn],
            recv_sem=piece_recv.at[leaf], device_id=(target, chan), device_id_type=MESH,
        )

    for turn in range(pieces):
        target, copy = piece_copy(turn)
        pl.when(target != leaf)(copy.start)

    take_chan(merged, merged_send, merged_recv)

    def fill_all(target, _):
        held = jnp.zeros((out_own, groups), jnp.float32)
        for source in range(chans):
            mine = owner[source : source + 1]
            held = held + jnp.where(mine == target, merged[source].astype(jnp.float32), 0.0)
        outbox[target] = held.astype(jnp.bfloat16)
        return 0

    lax.fori_loop(0, leaves, fill_all, 0, unroll=8)
    send_leaf(lambda peer: outbox.at[peer], inbox, box_send, box_recv)
    inbox[leaf] = outbox[leaf]

    @pl.when(leaf < pieces)
    def _():
        piece_in[leaf] = piece[leaf]
        take_leaf(piece_in, piece_send, piece_recv)

        def add(source, held):
            return held + piece_in[source]

        held = lax.fori_loop(1, leaves, add, piece_in[0], unroll=7 if leaves == 8 else 1)
        total[leaf] = held * (1.0 / math.sqrt(KIDS * group_count))
        each(leaves - 1, lambda turn: leaf_copy(
            lambda peer: total.at[leaf], total, total_send, total_recv, turn).start())

    take_leaf(inbox, box_send, box_recv)
    for tile in range(leaves // per_tile):
        whole = jnp.zeros((out_own, LANES), jnp.float32)
        for inside in range(per_tile):
            folded = inbox[tile * per_tile + inside].astype(jnp.float32)
            shift = pair_slots
            while shift < LANES:
                folded = folded + pltpu.roll(folded, shift, 1)
                shift *= 2
            whole = jnp.where(lane == inside, folded, whole)
        parents[:, pl.ds(tile * LANES, LANES)] = whole.astype(jnp.bfloat16)

    for index in range(pieces):
        arrival = pltpu.make_async_remote_copy(
            src_ref=total.at[index], dst_ref=total.at[index], send_sem=total_send.at[0],
            recv_sem=total_recv.at[index], device_id=(index, chan), device_id_type=MESH,
        )
        pl.when(leaf != index)(arrival.wait_recv)
    for index in range(pieces):
        row, kid = index // across * PIECE_ROWS, index % across * (LANES // width)
        summed = total[index]
        for inside in range(LANES // width):
            one_kid = summed[:, inside * width : (inside + 1) * width]
            grad[kid + inside, row : row + PIECE_ROWS, :] = one_kid

    pl.when(at_first & (leaf < leaves - 1))(from_left.wait_send)
    pl.when(at_last & (leaf > 0))(from_right.wait_send)
    for number, wait in sends:
        each(number, wait)
    for turn in range(pieces):
        target, copy = piece_copy(turn)
        pl.when(target != leaf)(copy.wait_send)

    @pl.when(leaf < pieces)
    def _():
        each(leaves - 1, lambda turn: leaf_copy(
            lambda peer: total.at[leaf], total, total_send, total_recv, turn).wait_send())


def per_device(features, neighbours, child_count, dest, conv_weight, merge_weight, parent_grad):
    width, row_count = features.shape
    taps = neighbours.shape[0]
    out_own = merge_weight.shape[2]
    group_count = row_count // KIDS
    leaves = lax.axis_size("leaf")
    chans = lax.axis_size("chan")
    quarter = row_count // chans
    groups = quarter // KIDS
    pieces = min(leaves, out_own * KIDS * width // (PIECE_ROWS * LANES))
    anywhere = pl.BlockSpec(memory_space=pl.ANY)
    whole = pl.BlockSpec(memory_space=pltpu.VMEM)
    scalars = pl.BlockSpec(memory_space=pltpu.SMEM)
    bf16, f32 = jnp.bfloat16, jnp.float32

    def sems(*counts):
        return [pltpu.SemaphoreType.DMA((count,)) for count in counts]

    parents, grad = pl.pallas_call(
        functools.partial(octree_kernel, chans, leaves),
        out_shape=(
            jax.ShapeDtypeStruct((out_own, group_count), bf16),
            jax.ShapeDtypeStruct((KIDS, out_own, width), f32),
        ),
        in_specs=[anywhere, anywhere, scalars] + [whole] * 4,
        out_specs=(whole, whole),
        scratch_shapes=[
            pltpu.VMEM((width, quarter + 2 * HALO), bf16),
            pltpu.VMEM((taps, quarter), jnp.int32),
            pltpu.VMEM((chans, width // chans, taps * width), bf16),
            pltpu.VMEM((chans, out_own, KIDS * width), bf16),
            pltpu.VMEM((leaves, out_own, groups), bf16),
            pltpu.VMEM((leaves, out_own, groups), bf16),
            pltpu.VMEM((chans, out_own, groups), bf16),
            pltpu.VMEM((chans, out_own, groups), bf16),
            pltpu.VMEM((taps * width, BLOCK), bf16),
            pltpu.VMEM((KIDS * width, groups), bf16),
            pltpu.VMEM((chans, out_own, groups), bf16),
            pltpu.VMEM((chans, out_own, groups), bf16),
            pltpu.VMEM((leaves, out_own, groups), bf16),
            pltpu.VMEM((leaves, out_own, groups), bf16),
            pltpu.VMEM((chans, out_own, KIDS * width), f32),
            pltpu.VMEM((chans, out_own, KIDS * width), bf16),
            pltpu.VMEM((chans, out_own, KIDS * width), bf16),
            pltpu.VMEM((pieces, PIECE_ROWS, LANES), f32),
            pltpu.VMEM((leaves, PIECE_ROWS, LANES), f32),
            pltpu.VMEM((pieces, PIECE_ROWS, LANES), f32),
        ]
        + sems(4, 2, 2)
        + sems(chans, chans, chans, chans)
        + sems(leaves, leaves)
        + sems(chans, chans, chans, chans)
        + sems(leaves, leaves)
        + sems(chans, chans)
        + sems(pieces, leaves)
        + sems(leaves, leaves),
        compiler_params=pltpu.CompilerParams(
            collective_id=0, has_side_effects=True, vmem_limit_bytes=40 * 1024 * 1024
        ),
    )(
        features,
        neighbours,
        child_count,
        dest.reshape(chans, groups),
        conv_weight.swapaxes(1, 2),
        merge_weight.swapaxes(1, 2),
        parent_grad,
    )
    return (parents, grad.swapaxes(1, 2))


def solution(mesh):
    in_specs = (
        P(None, "leaf"),
        P(None, "leaf"),
        P("leaf"),
        P("leaf"),
        P(None, None, "chan"),
        P(None, None, "chan"),
        P("chan", "leaf"),
    )
    out_specs = (P("chan", "leaf"), P(None, None, "chan"))
    return jax.shard_map(
        per_device, mesh=mesh, in_specs=in_specs, out_specs=out_specs, check_vma=False
    )
```

```python
import functools
import math

import jax
import jax.numpy as jnp
from jax import lax
from jax.experimental import pallas as pl
from jax.experimental.pallas import tpu as pltpu
from jax.sharding import PartitionSpec as P

KIDS = 8
HALO = 1024
LO = 256
BLOCK = 256
REACH = (2 * HALO + BLOCK) // LO
LANES = 128
PIECE_ROWS = 16
MESH = pl.DeviceIdType.MESH


def each(count, step):
    if count <= 8:
        for turn in range(count):
            step(turn)
    else:
        lax.fori_loop(0, count, lambda turn, _: (step(turn), 0)[1], 0)


def octree_kernel(
    chans,
    leaves,
    features,
    neighbours,
    child_count,
    dest_far,
    conv_far,
    merge_far,
    cotangent_far,
    parents_far,
    grad_far,
    dest,
    conv_own,
    merge_own,
    cotangent_own,
    parents,
    grad,
    window,
    offsets,
    conv,
    merge,
    cotangent,
    backward,
    fetched_out,
    fetched,
    picked,
    stacked,
    merged_out,
    merged,
    outbox,
    inbox,
    part,
    part_out,
    part_in,
    piece,
    piece_in,
    total,
    local_sem,
    halo_send,
    halo_recv,
    conv_send,
    conv_recv,
    merge_send,
    merge_recv,
    back_send,
    back_recv,
    fetched_send,
    fetched_recv,
    merged_send,
    merged_recv,
    box_send,
    box_recv,
    part_send,
    part_recv,
    piece_send,
    piece_recv,
    total_send,
    total_recv,
):
    leaf = lax.axis_index("leaf")
    chan = lax.axis_index("chan")
    width, row_count = features.shape
    taps = neighbours.shape[0]
    quarter = row_count // chans
    groups = quarter // KIDS
    group_count = row_count // KIDS
    pair_slots = group_count // leaves
    out_own = merge_own.shape[1]
    pieces = piece.shape[0]
    first_row = pl.multiple_of(chan * quarter, LO)

    def chan_copy(src, dst, send, recv, turn):
        peer = lax.rem(chan + turn + 1, chans)
        return pltpu.make_async_remote_copy(
            src_ref=src(peer), dst_ref=dst.at[chan], send_sem=send.at[turn],
            recv_sem=recv.at[chan], device_id=(leaf, peer), device_id_type=MESH,
        )

    def chan_arrival(dst, send, recv, turn):
        peer = lax.rem(chan + turn + 1, chans)
        return pltpu.make_async_remote_copy(
            src_ref=dst.at[peer], dst_ref=dst.at[peer], send_sem=send.at[turn],
            recv_sem=recv.at[peer], device_id=(leaf, peer), device_id_type=MESH,
        )

    def leaf_copy(src, dst, send, recv, turn):
        peer = lax.rem(leaf + turn + 1, leaves)
        return pltpu.make_async_remote_copy(
            src_ref=src(peer), dst_ref=dst.at[leaf], send_sem=send.at[turn],
            recv_sem=recv.at[leaf], device_id=(peer, chan), device_id_type=MESH,
        )

    def leaf_arrival(dst, send, recv, turn):
        peer = lax.rem(leaf + turn + 1, leaves)
        return pltpu.make_async_remote_copy(
            src_ref=dst.at[peer], dst_ref=dst.at[peer], send_sem=send.at[turn],
            recv_sem=recv.at[peer], device_id=(peer, chan), device_id_type=MESH,
        )

    def near(at, size):
        return features.at[:, pl.ds(at, size)]

    left_local = pltpu.make_async_copy(
        near(pl.multiple_of(jnp.maximum(first_row - HALO, 0), LO), HALO),
        window.at[:, pl.ds(0, HALO)], local_sem.at[0],
    )
    right_local = pltpu.make_async_copy(
        near(pl.multiple_of(jnp.minimum(first_row + quarter, row_count - HALO), LO), HALO),
        window.at[:, pl.ds(HALO + quarter, HALO)], local_sem.at[1],
    )
    centre_local = pltpu.make_async_copy(
        near(first_row, quarter), window.at[:, pl.ds(HALO, quarter)], local_sem.at[2]
    )
    offsets_local = pltpu.make_async_copy(
        neighbours.at[:, pl.ds(first_row, quarter)], offsets, local_sem.at[3]
    )
    from_left = pltpu.make_async_remote_copy(
        src_ref=near(row_count - HALO, HALO), dst_ref=window.at[:, pl.ds(0, HALO)],
        send_sem=halo_send.at[0], recv_sem=halo_recv.at[0],
        device_id=(jnp.minimum(leaf + 1, leaves - 1), chan), device_id_type=MESH,
    )
    from_right = pltpu.make_async_remote_copy(
        src_ref=near(0, HALO), dst_ref=window.at[:, pl.ds(HALO + quarter, HALO)],
        send_sem=halo_send.at[1], recv_sem=halo_recv.at[1],
        device_id=(jnp.maximum(leaf - 1, 0), chan), device_id_type=MESH,
    )
    at_first = chan == 0
    at_last = chan == chans - 1

    owned = [
        pltpu.make_async_copy(far, close, local_sem.at[4 + number])
        for number, (far, close) in enumerate(
            ((conv_far, conv_own), (cotangent_far, cotangent_own), (merge_far, merge_own), (dest_far, dest))
        )
    ]
    for copy in owned:
        copy.start()
    offsets_local.start()
    centre_local.start()
    pl.when(jnp.logical_not(at_first))(left_local.start)
    pl.when(jnp.logical_not(at_last))(right_local.start)

    barrier = pltpu.get_barrier_semaphore()

    def greet_chan(turn):
        peer = lax.rem(chan + turn + 1, chans)
        pl.semaphore_signal(barrier, inc=1, device_id=(leaf, peer), device_id_type=MESH)

    def greet_leaf(turn):
        peer = lax.rem(leaf + turn + 1, leaves)
        pl.semaphore_signal(barrier, inc=1, device_id=(peer, chan), device_id_type=MESH)

    each(chans - 1, greet_chan)
    each(leaves - 1, greet_leaf)

    for copy in owned:
        copy.wait()
    for tap in range(0, taps, 2):
        beside = jnp.concatenate([conv_own[at] for at in range(tap, min(tap + 2, taps))], axis=1)
        conv[chan, :, tap * width : tap * width + beside.shape[1]] = beside
    for kid in range(0, KIDS, 2):
        beside = jnp.concatenate([merge_own[kid], merge_own[kid + 1]], axis=1)
        merge[chan, :, kid * width : (kid + 2) * width] = beside
    lane = lax.broadcasted_iota(jnp.int32, (1, LANES), 1) // pair_slots
    per_tile = LANES // pair_slots
    for tile in range(leaves // per_tile):
        held = cotangent_own[:, tile * LANES : (tile + 1) * LANES].astype(jnp.float32)
        for inside in range(per_tile):
            spread = jnp.where(lane == inside, held, 0.0)
            shift = pair_slots
            while shift < LANES:
                spread = spread + pltpu.roll(spread, shift, 1)
                shift *= 2
            cotangent[tile * per_tile + inside] = spread.astype(jnp.bfloat16)

    pl.semaphore_wait(barrier, chans + leaves - 2)

    pl.when(at_first & (leaf < leaves - 1))(from_left.start)
    pl.when(at_last & (leaf > 0))(from_right.start)
    sends = []

    def send_chan(src, dst, send, recv):
        each(chans - 1, lambda turn: chan_copy(src, dst, send, recv, turn).start())
        sends.append((chans - 1, lambda turn: chan_copy(src, dst, send, recv, turn).wait_send()))

    def send_leaf(src, dst, send, recv):
        each(leaves - 1, lambda turn: leaf_copy(src, dst, send, recv, turn).start())
        sends.append((leaves - 1, lambda turn: leaf_copy(src, dst, send, recv, turn).wait_send()))

    def take_chan(dst, send, recv):
        each(chans - 1, lambda turn: chan_arrival(dst, send, recv, turn).wait_recv())

    def take_leaf(dst, send, recv):
        each(leaves - 1, lambda turn: leaf_arrival(dst, send, recv, turn).wait_recv())

    send_chan(lambda peer: conv.at[chan], conv, conv_send, conv_recv)
    send_leaf(lambda peer: cotangent.at[peer], backward, back_send, back_recv)
    send_chan(lambda peer: merge.at[chan], merge, merge_send, merge_recv)
    backward[leaf] = cotangent[leaf]

    @pl.when(at_first & (leaf == 0))
    def _():
        window[:, :HALO] = jnp.zeros((width, HALO), jnp.bfloat16)

    @pl.when(at_last & (leaf == leaves - 1))
    def _():
        window[:, HALO + quarter :] = jnp.zeros((width, HALO), jnp.bfloat16)

    offsets_local.wait()
    centre_local.wait()
    pl.when(jnp.logical_not(at_first))(left_local.wait)
    pl.when(jnp.logical_not(at_last))(right_local.wait)

    slot = lax.broadcasted_iota(jnp.int32, (LO, BLOCK), 0).astype(jnp.float32).astype(jnp.bfloat16)
    local = lax.broadcasted_iota(jnp.int32, (1, BLOCK), 1)
    count = child_count[0]

    blocks = quarter // BLOCK
    centre = taps // 2
    flip = jnp.where(at_first, 1, 0)

    def block_of(turn):
        return jnp.where(at_first, blocks - 1 - turn, turn)

    def span_of(block):
        return pl.ds(pl.multiple_of(block * BLOCK, BLOCK), BLOCK)

    def chunk_at(number):
        return window[:, pl.ds(pl.multiple_of(number * LO, LO), LO)]

    def over_taps(step):
        for low, high in ((0, centre), (centre + 1, taps)):
            lax.fori_loop(low, high, lambda tap, _: (step(tap), 0)[1], 0, unroll=high - low)

    def split(tap, block):
        offset = offsets[pl.ds(tap, 1), span_of(block)]
        place = local + offset
        chunk = place // LO
        inner = jnp.where(offset >= 0, place - chunk * LO, -1)
        inner = inner.astype(jnp.float32).astype(jnp.bfloat16)
        return chunk, jnp.where(slot == inner, jnp.bfloat16(1), jnp.bfloat16(0))

    def tap_rows(tap):
        return pl.ds(pl.multiple_of(tap * width, width), width)

    def own_rows(block):
        picked[pl.ds(centre * width, width), :] = chunk_at(block + HALO // LO)

    def pick(block):
        own_rows(block)
        source = jnp.concatenate([chunk_at(block + high) for high in range(REACH)], axis=0)

        def one(tap):
            chunk, hot = split(tap, block)
            found = jnp.dot(source, hot, preferred_element_type=jnp.float32)
            taken = found[:width]
            for high in range(1, REACH):
                taken = jnp.where(chunk == high, found[high * width : (high + 1) * width], taken)
            picked[tap_rows(tap), :] = taken.astype(jnp.bfloat16)

        over_taps(one)

    def pick_local(block):
        first = block + flip
        own_rows(block)
        source = jnp.concatenate([chunk_at(first + high) for high in range(REACH - 1)], axis=0)

        def one(tap):
            chunk, hot = split(tap, block)
            found = jnp.dot(source, hot, preferred_element_type=jnp.float32)
            taken = jnp.zeros((width, BLOCK), jnp.float32)
            for high in range(REACH - 1):
                here = chunk == high + flip
                taken = jnp.where(here, found[high * width : (high + 1) * width], taken)
            picked[tap_rows(tap), :] = taken.astype(jnp.bfloat16)

        over_taps(one)

    def pick_halo(block):
        far = (REACH - 1) * (1 - flip)
        source = chunk_at(block + far)

        def one(tap):
            chunk, hot = split(tap, block)
            found = jnp.dot(source, hot, preferred_element_type=jnp.float32)
            held = picked[tap_rows(tap), :].astype(jnp.float32)
            picked[tap_rows(tap), :] = jnp.where(chunk == far, found, held).astype(jnp.bfloat16)

        over_taps(one)

    def convolve(block, fresh):
        weight = conv[...].reshape(width, taps * width)
        pre_act = jnp.dot(weight, picked[...], preferred_element_type=jnp.float32)
        living = first_row + block * BLOCK + local < count
        hidden = jnp.where(living, jnp.maximum(pre_act, 0.0), 0.0).astype(jnp.bfloat16)
        kids = BLOCK // groups
        for kid in range(0, KIDS, kids):
            wanted = lax.broadcasted_iota(jnp.int32, (1, BLOCK), 1)
            wanted = wanted % groups * KIDS + kid + wanted // groups - block * BLOCK
            wanted = jnp.where((wanted >= 0) & (wanted < BLOCK), wanted, -1)
            wanted = wanted.astype(jnp.float32).astype(jnp.bfloat16)
            order = jnp.where(slot == wanted, jnp.bfloat16(1), jnp.bfloat16(0))
            moved = jnp.dot(hidden, order, preferred_element_type=jnp.float32).astype(jnp.bfloat16)
            for inside in range(kids):
                rows = pl.ds((kid + inside) * width, width)
                new = moved[:, inside * groups : (inside + 1) * groups]
                stacked[rows, :] = new if fresh else stacked[rows, :] + new

    pick_local(block_of(0))
    pl.when(at_first & (leaf > 0))(from_left.wait_recv)
    pl.when(at_last & (leaf < leaves - 1))(from_right.wait_recv)
    pick_halo(block_of(0))
    take_chan(conv, conv_send, conv_recv)
    convolve(block_of(0), True)

    take_leaf(backward, back_send, back_recv)
    owner = dest[...] // group_count
    for part_index in range(chans):
        mine = owner[part_index : part_index + 1]

        def gain(source, held):
            return jnp.where(mine == source, backward[source].astype(jnp.float32), held)

        nothing = jnp.zeros((out_own, groups), jnp.float32)
        held = lax.fori_loop(0, leaves, gain, nothing, unroll=8)
        fetched_out[part_index] = held.astype(jnp.bfloat16)
    send_chan(lambda peer: fetched_out.at[peer], fetched, fetched_send, fetched_recv)
    fetched[chan] = fetched_out[chan]

    for turn in range(1, blocks):
        pick(block_of(turn))
        convolve(block_of(turn), False)

    take_chan(fetched, fetched_send, fetched_recv)
    part[...] = lax.dot_general(
        fetched[...].reshape(chans * out_own, groups), stacked[...],
        (((1,), (1,)), ((), ())), preferred_element_type=jnp.float32,
    ).reshape(part.shape)
    part_out[...] = part[...].astype(jnp.bfloat16)
    send_chan(lambda peer: part_out.at[peer], part_in, part_send, part_recv)

    take_chan(merge, merge_send, merge_recv)
    merged_out[...] = jnp.dot(
        merge[...].reshape(chans * out_own, KIDS * width), stacked[...],
        preferred_element_type=jnp.float32,
    ).astype(jnp.bfloat16).reshape(merged_out.shape)
    send_chan(lambda peer: merged_out.at[peer], merged, merged_send, merged_recv)
    merged[chan] = merged_out[chan]

    take_chan(part_in, part_send, part_recv)
    term = part[chan]
    for turn in range(1, chans):
        term = term + part_in[lax.rem(chan + turn, chans)].astype(jnp.float32)
    across = KIDS * width // LANES
    for index in range(pieces):
        row, column = index // across * PIECE_ROWS, index % across * LANES
        piece[index] = term[row : row + PIECE_ROWS, column : column + LANES]

    def piece_copy(turn):
        target = lax.rem(leaf + turn, pieces)
        return target, pltpu.make_async_remote_copy(
            src_ref=piece.at[target], dst_ref=piece_in.at[leaf], send_sem=piece_send.at[turn],
            recv_sem=piece_recv.at[leaf], device_id=(target, chan), device_id_type=MESH,
        )

    for turn in range(pieces):
        target, copy = piece_copy(turn)
        pl.when(target != leaf)(copy.start)

    take_chan(merged, merged_send, merged_recv)

    def fill_all(target, _):
        held = jnp.zeros((out_own, groups), jnp.float32)
        for source in range(chans):
            mine = owner[source : source + 1]
            held = held + jnp.where(mine == target, merged[source].astype(jnp.float32), 0.0)
        outbox[target] = held.astype(jnp.bfloat16)
        return 0

    lax.fori_loop(0, leaves, fill_all, 0, unroll=8)
    send_leaf(lambda peer: outbox.at[peer], inbox, box_send, box_recv)
    inbox[leaf] = outbox[leaf]

    @pl.when(leaf < pieces)
    def _():
        piece_in[leaf] = piece[leaf]
        take_leaf(piece_in, piece_send, piece_recv)

        def add(source, held):
            return held + piece_in[source]

        held = lax.fori_loop(1, leaves, add, piece_in[0], unroll=7 if leaves == 8 else 1)
        total[leaf] = held * (1.0 / math.sqrt(KIDS * group_count))
        each(leaves - 1, lambda turn: leaf_copy(
            lambda peer: total.at[leaf], total, total_send, total_recv, turn).start())

    take_leaf(inbox, box_send, box_recv)
    for tile in range(leaves // per_tile):
        whole = jnp.zeros((out_own, LANES), jnp.float32)
        for inside in range(per_tile):
            folded = inbox[tile * per_tile + inside].astype(jnp.float32)
            shift = pair_slots
            while shift < LANES:
                folded = folded + pltpu.roll(folded, shift, 1)
                shift *= 2
            whole = jnp.where(lane == inside, folded, whole)
        parents[:, pl.ds(tile * LANES, LANES)] = whole.astype(jnp.bfloat16)
    parents_done = pltpu.make_async_copy(parents, parents_far, local_sem.at[8])
    parents_done.start()

    for index in range(pieces):
        arrival = pltpu.make_async_remote_copy(
            src_ref=total.at[index], dst_ref=total.at[index], send_sem=total_send.at[0],
            recv_sem=total_recv.at[index], device_id=(index, chan), device_id_type=MESH,
        )
        pl.when(leaf != index)(arrival.wait_recv)
    for index in range(pieces):
        row, kid = index // across * PIECE_ROWS, index % across * (LANES // width)
        summed = total[index]
        for inside in range(LANES // width):
            one_kid = summed[:, inside * width : (inside + 1) * width]
            grad[kid + inside, row : row + PIECE_ROWS, :] = one_kid
    grad_done = pltpu.make_async_copy(grad, grad_far, local_sem.at[9])
    grad_done.start()

    pl.when(at_first & (leaf < leaves - 1))(from_left.wait_send)
    pl.when(at_last & (leaf > 0))(from_right.wait_send)
    for number, wait in sends:
        each(number, wait)
    for turn in range(pieces):
        target, copy = piece_copy(turn)
        pl.when(target != leaf)(copy.wait_send)

    @pl.when(leaf < pieces)
    def _():
        each(leaves - 1, lambda turn: leaf_copy(
            lambda peer: total.at[leaf], total, total_send, total_recv, turn).wait_send())
    parents_done.wait()
    grad_done.wait()


def settle_kernel(parents, grad, parents_out, grad_out, sem):
    copies = (
        pltpu.make_async_copy(parents, parents_out, sem.at[0]),
        pltpu.make_async_copy(grad, grad_out, sem.at[1]),
    )
    for copy in copies:
        copy.start()
    for copy in copies:
        copy.wait()


def per_device(features, neighbours, child_count, dest, conv_weight, merge_weight, parent_grad):
    width, row_count = features.shape
    taps = neighbours.shape[0]
    out_own = merge_weight.shape[2]
    group_count = row_count // KIDS
    leaves = lax.axis_size("leaf")
    chans = lax.axis_size("chan")
    quarter = row_count // chans
    groups = quarter // KIDS
    pieces = min(leaves, out_own * KIDS * width // (PIECE_ROWS * LANES))
    anywhere = pl.BlockSpec(memory_space=pl.ANY)
    scalars = pl.BlockSpec(memory_space=pltpu.SMEM)
    bf16, f32 = jnp.bfloat16, jnp.float32

    def sems(*counts):
        return [pltpu.SemaphoreType.DMA((count,)) for count in counts]

    parents, grad = pl.pallas_call(
        functools.partial(octree_kernel, chans, leaves),
        out_shape=(
            jax.ShapeDtypeStruct((out_own, group_count), bf16),
            jax.ShapeDtypeStruct((KIDS, out_own, width), f32),
        ),
        in_specs=[anywhere, anywhere, scalars] + [anywhere] * 4,
        out_specs=(anywhere, anywhere),
        scratch_shapes=[
            pltpu.VMEM((chans, groups), jnp.int32),
            pltpu.VMEM((taps, width // chans, width), bf16),
            pltpu.VMEM((KIDS, out_own, width), bf16),
            pltpu.VMEM((out_own, group_count), bf16),
            pltpu.VMEM((out_own, group_count), bf16),
            pltpu.VMEM((KIDS, out_own, width), f32),
            pltpu.VMEM((width, quarter + 2 * HALO), bf16),
            pltpu.VMEM((taps, quarter), jnp.int32),
            pltpu.VMEM((chans, width // chans, taps * width), bf16),
            pltpu.VMEM((chans, out_own, KIDS * width), bf16),
            pltpu.VMEM((leaves, out_own, groups), bf16),
            pltpu.VMEM((leaves, out_own, groups), bf16),
            pltpu.VMEM((chans, out_own, groups), bf16),
            pltpu.VMEM((chans, out_own, groups), bf16),
            pltpu.VMEM((taps * width, BLOCK), bf16),
            pltpu.VMEM((KIDS * width, groups), bf16),
            pltpu.VMEM((chans, out_own, groups), bf16),
            pltpu.VMEM((chans, out_own, groups), bf16),
            pltpu.VMEM((leaves, out_own, groups), bf16),
            pltpu.VMEM((leaves, out_own, groups), bf16),
            pltpu.VMEM((chans, out_own, KIDS * width), f32),
            pltpu.VMEM((chans, out_own, KIDS * width), bf16),
            pltpu.VMEM((chans, out_own, KIDS * width), bf16),
            pltpu.VMEM((pieces, PIECE_ROWS, LANES), f32),
            pltpu.VMEM((leaves, PIECE_ROWS, LANES), f32),
            pltpu.VMEM((pieces, PIECE_ROWS, LANES), f32),
        ]
        + sems(10, 2, 2)
        + sems(chans, chans, chans, chans)
        + sems(leaves, leaves)
        + sems(chans, chans, chans, chans)
        + sems(leaves, leaves)
        + sems(chans, chans)
        + sems(pieces, leaves)
        + sems(leaves, leaves),
        compiler_params=pltpu.CompilerParams(
            collective_id=0, has_side_effects=True, vmem_limit_bytes=56 * 1024 * 1024
        ),
    )(
        features,
        neighbours,
        child_count,
        dest.reshape(chans, groups),
        conv_weight.swapaxes(1, 2),
        merge_weight.swapaxes(1, 2),
        parent_grad,
    )
    parents, grad = pl.pallas_call(
        settle_kernel,
        out_shape=(
            jax.ShapeDtypeStruct(parents.shape, bf16),
            jax.ShapeDtypeStruct(grad.shape, f32),
        ),
        in_specs=[anywhere] * 2,
        out_specs=(anywhere, anywhere),
        scratch_shapes=sems(2),
        compiler_params=pltpu.CompilerParams(vmem_limit_bytes=56 * 1024 * 1024),
    )(parents, grad)
    return (parents, grad.swapaxes(1, 2))


def solution(mesh):
    in_specs = (
        P(None, "leaf"),
        P(None, "leaf"),
        P("leaf"),
        P("leaf"),
        P(None, None, "chan"),
        P(None, None, "chan"),
        P("chan", "leaf"),
    )
    out_specs = (P("chan", "leaf"), P(None, None, "chan"))
    return jax.shard_map(
        per_device, mesh=mesh, in_specs=in_specs, out_specs=out_specs, check_vma=False
    )
```
